256 devices in a mesh: row: 16 (over y, x), col: 16 (over z, core).
Axes of the slice: x: 4, y: 4, z: 8, core: 2. Of those that a mesh axis runs over, the one named last changes fastest.
Arguments:
- matrix: float32 [24576, 16384], P('row', 'col'), may hold values from -6 to 6
- lower_panel: float32 [256, 24576], P('col', 'row'), may hold values from -0.375 to 0.375
- pivots: int32 [256], replicated, may hold values from 256 to 24575, as said below
Outputs:
- updated: float32 [24576, 16384], P('row', 'col')
The draws below stay inside these ranges and needn't reach their ends.
Inputs may be any that keep to these rules, and one draw needn't show every extreme that they name: `pivots`: distinct row ids, each at least 256; the largest and smallest allowed values occur in every draw.
All inputs are finite; a program needn't handle non-finite values.
Results may differ from the reference program's by a relative error of at most 0.0001.
Values sent between devices are 32-bit elements; how exact they have to be, the bound alone decides.
A program may use at most 64 MiB of HBM per device.

```python
import jax
import jax.numpy as jnp
from jax import lax

NB = 256
NT = 16384
ROWS_DEV = 1536
M = 24576
N_ROW = 16


def draw_pivots(key, part):
    key = jax.random.fold_in(key, 7)
    shuffled = jax.random.permutation(key, M - NB)[:NB] + NB
    shuffled = jnp.where(shuffled == jnp.max(shuffled), M - 1, shuffled)
    shuffled = jnp.where(shuffled == jnp.min(shuffled), NB, shuffled)
    return shuffled.astype(jnp.int32)


def shard_levels(stream_key, shape, cuts, low, high):
    gain = 1.0
    for axis_at, shards_of in cuts:
        steps = jax.random.uniform(jax.random.fold_in(jax.random.fold_in(stream_key, 6), axis_at), (shards_of,), jnp.float32, low / len(cuts), high / len(cuts))
        gain = gain * jnp.repeat(jnp.exp(steps), shape[axis_at] // shards_of).reshape((-1,) + (1,) * (len(shape) - 1 - axis_at))
    return gain


def normal_values(own_key, extent, width, bound, split=(), kind=jnp.bfloat16):
    loudness = shard_levels(own_key, extent, split, -0.22, 0.18) if split else 1.0
    array = jax.random.normal(own_key, extent, jnp.float32) * width * loudness
    return jnp.minimum(jnp.maximum(array, -bound), bound).astype(kind)


def setup_inputs(seed: int = 0) -> dict:
    key_list = jax.random.split(jax.random.key(seed), 4)
    return {
        "matrix": normal_values(key_list[0], (M, NT), 1.0, 6.0, ((0, 16), (1, 16)), jnp.float32),
        "lower_panel": normal_values(key_list[1], (NB, M), NB ** -0.5, 0.375, ((0, 16), (1, 16)), jnp.float32),
        "pivots": draw_pivots(jax.random.fold_in(key_list[3], 71), 0),
    }


def multiply(left_side, right_side):
    return jnp.dot(left_side, right_side, preferred_element_type=jnp.float32, precision=lax.Precision.HIGHEST)


def block_inverse(diag_block):
    strict = jnp.tril(diag_block, -1)
    identity = jnp.eye(diag_block.shape[0], dtype=jnp.float32)
    result = identity - strict
    powered = strict
    for repeat in range(4):
        powered = multiply(powered, powered)
        result = multiply(result, identity + powered)
    return result


def unit_lower_solve(triangle, right_side):
    block_rows = 32
    solved = []
    for offset in range(0, triangle.shape[0], block_rows):
        target = right_side[offset:offset + block_rows]
        if offset > 0:
            target = target - multiply(triangle[offset:offset + block_rows, :offset], jnp.concatenate(solved, axis=0))
        solved.append(multiply(block_inverse(triangle[offset:offset + block_rows, offset:offset + block_rows]), target))
    return jnp.concatenate(solved, axis=0)


def reference(matrix, lower_panel, pivots):
    top_index = jnp.arange(NB, dtype=jnp.int32)
    pivot_ids = pivots.astype(jnp.int32)
    touched = jnp.concatenate([top_index, pivot_ids])
    sources = jnp.concatenate([pivot_ids, top_index])
    swapped = matrix.at[touched].set(matrix[sources])
    triangle = jnp.transpose(lower_panel[:, :NB])
    u_rows = unit_lower_solve(triangle, swapped[:NB])
    blocks = swapped.reshape(N_ROW, ROWS_DEV, NT)
    panels = jnp.transpose(lower_panel.reshape(NB, N_ROW, ROWS_DEV), (1, 0, 2))

    def update_block(pair):
        return pair[0] - lax.dot_general(pair[1], u_rows, (((0,), (0,)), ((), ())), precision=lax.Precision.HIGHEST, preferred_element_type=jnp.float32)

    updated = lax.map(update_block, (blocks, panels)).reshape(N_ROW * ROWS_DEV, NT)
    return updated.at[:NB].set(u_rows)
```

```python
import jax
import jax.numpy as jnp
from jax import lax
from jax.experimental import pallas as pl
from jax.experimental.pallas import tpu as pltpu
from jax.sharding import PartitionSpec as P

NB = 256
ROWS = 1536
COLS = 1024
HALF = 512
MESH = pl.DeviceIdType.MESH
F32 = jnp.float32
BF16 = jnp.bfloat16


def exact(a, b):
    return jnp.dot(a, b, preferred_element_type=F32, precision=lax.Precision.HIGHEST)


def upper_inverse(tri):
    i = lax.broadcasted_iota(jnp.int32, (NB, NB), 0)
    j = lax.broadcasted_iota(jnp.int32, (NB, NB), 1)
    eye = jnp.where(i == j, 1.0, 0.0).astype(F32)
    power = jnp.where((j > i) & (i // 32 == j // 32), tri, 0.0)
    inv = eye - power
    for _ in range(4):
        power = exact(power, power)
        inv = exact(inv, eye + power)
    for size in (32, 64, 128):
        block = (i // (2 * size) == j // (2 * size)) & (i // size < j // size)
        inv = inv - exact(exact(inv, jnp.where(block, tri, 0.0)), inv)
    return inv


def exchange_kernel(
    piv, mat_hbm, panel, top, old, w_hi, w_lo,
    mat, sel, r1a, r1b, r2a, r2b, pa, pb, pan, tri, inv,
    mat_sem, p1s, p1r, p2s, p2r, p3s, p3r, p4s, p4r, scs, scr, tbs, tbr,
    tzs, tzr, tcs, tcr, pzs, pzr, pcs, pcr,
):
    r = lax.axis_index("row")
    c = lax.axis_index("col")
    y, x = r // 4, r % 4
    z, k = c // 2, c % 2
    is_root = r == 0

    head = pltpu.make_async_copy(mat_hbm.at[pl.ds(0, NB)], mat.at[pl.ds(0, NB)], mat_sem.at[0])
    rest = pltpu.make_async_copy(mat_hbm.at[pl.ds(NB, ROWS - NB)], mat.at[pl.ds(NB, ROWS - NB)], mat_sem.at[1])
    head.start()
    rest.start()

    def rowdev(yy, xx):
        return (yy * 4 + xx, c)

    def coldev(zz, kk):
        return (r, zz * 2 + kk)

    barrier = pltpu.get_barrier_semaphore()
    for d in range(1, 16):
        pl.semaphore_signal(barrier, inc=1, device_id=((r + d) % 16, c), device_id_type=MESH)
    for d in range(1, 8):
        pl.semaphore_signal(barrier, inc=1, device_id=coldev((z + d) % 8, k), device_id_type=MESH)
    pl.semaphore_signal(barrier, inc=1, device_id=coldev(z, 1 - k), device_id_type=MESH)
    pl.semaphore_wait(barrier, 23)

    def remote(src, dst, ss, rs, dev):
        return pltpu.make_async_remote_copy(
            src_ref=src, dst_ref=dst, send_sem=ss, recv_sem=rs, device_id=dev, device_id_type=MESH
        )

    def piece(ref, zz, kk):
        return ref.at[pl.ds(pl.multiple_of((zz * 2 + kk) * 16, 16), 16)]

    mine = piece(tri, z, k)
    tri_bcast = [
        remote(panel.at[:, pl.ds(0, NB)], mine, tbs.at[d - 1], tbr.at[0], ((r + d) % 16, c)) for d in range(1, 16)
    ]

    @pl.when(is_root)
    def _():
        for cp in tri_bcast:
            cp.start()
        tri[pl.ds(pl.multiple_of(c * 16, 16), 16), :] = panel[:, :NB]

    pan[pl.ds(pl.multiple_of(c * 16, 16), 16), :] = panel[...]
    pan_z = [
        remote(panel, piece(pan, z, k), pzs.at[d - 1], pzr.at[d - 1], coldev((z + d) % 8, k)) for d in range(1, 8)
    ]
    pan_core = [
        remote(
            panel if d == 0 else piece(pan, (z + 8 - d) % 8, k),
            piece(pan, (z + 8 - d) % 8, k),
            pcs.at[d], pcr.at[d], coldev(z, 1 - k),
        )
        for d in range(8)
    ]
    order = (1, 7, 2, 6, 3, 5, 4)
    for d in order:
        pan_z[d - 1].start()
    pan_core[0].start()

    head.wait()
    ca = pl.ds(0, HALF)
    cb = pl.ds(HALF, HALF)

    def rows_a(yy, xx):
        return pl.ds(pl.multiple_of(xx * 64 + yy * 16, 16), 16)

    def rows_b(yy, xx):
        return pl.ds(pl.multiple_of(yy * 64 + xx * 16, 16), 16)

    scatter = []
    for d in range(1, 16):
        rr = (r + d) % 16
        yy, xx = rr // 4, rr % 4
        at = (rows_a(yy, xx), ca)
        bt = (rows_b(yy, xx), cb)
        scatter.append(remote(mat.at[at], old.at[at], scs.at[2 * d - 2], scr.at[0], (rr, c)))
        scatter.append(remote(mat.at[bt], old.at[bt], scs.at[2 * d - 1], scr.at[1], (rr, c)))

    @pl.when(is_root)
    def _():
        for cp in scatter:
            cp.start()
        old[rows_a(y, x), ca] = mat[rows_a(y, x), ca]
        old[rows_b(y, x), cb] = mat[rows_b(y, x), cb]

    rest.wait()
    first = r * ROWS

    def pick(g, carry):
        for i in range(8):
            off = piv[g * 8 + i] - first
            own = (off >= 0) & (off < ROWS)
            row = mat[pl.ds(jnp.clip(off, 0, ROWS - 1), 1), :]
            sel[pl.ds(g * 8 + i, 1), :] = jnp.where(own, row, 0.0)
        return carry

    lax.fori_loop(0, NB // 8, pick, 0)

    def r64(i):
        return pl.ds(pl.multiple_of(i * 64, 64), 64)

    def r16(i):
        return pl.ds(pl.multiple_of(i * 16, 16), 16)

    p1 = []
    for d in (1, 3, 2):
        xx, yy = (x + d) % 4, (y + d) % 4
        p1.append(remote(sel.at[r64(xx), ca], r1a.at[d - 1], p1s.at[d - 1], p1r.at[d - 1], rowdev(y, xx)))
        p1.append(remote(sel.at[r64(yy), cb], r1b.at[d - 1], p1s.at[d + 2], p1r.at[d + 2], rowdev(yy, x)))
    for cp in p1:
        cp.start()

    tri_z = [
        remote(mine, mine, tzs.at[d - 1], tzr.at[d - 1], coldev((z + d) % 8, k)) for d in range(1, 8)
    ]
    tri_core = [
        remote(
            piece(tri, (z + 8 - d) % 8, k), piece(tri, (z + 8 - d) % 8, k),
            tcs.at[d], tcr.at[d], coldev(z, 1 - k),
        )
        for d in range(8)
    ]

    @pl.when(jnp.logical_not(is_root))
    def _():
        tri_bcast[0].wait_recv()

    for d in order:
        tri_z[d - 1].start()
    tri_core[0].start()

    for cp in p1:
        cp.wait_recv()
    pa[...] = sel[r64(x), ca] + r1a[0] + r1a[1] + r1a[2]
    pb[...] = sel[r64(y), cb] + r1b[0] + r1b[1] + r1b[2]
    p2 = []
    for d in (1, 3, 2):
        xx, yy = (x + d) % 4, (y + d) % 4
        p2.append(remote(pa.at[r16(yy)], r2a.at[d - 1], p2s.at[d - 1], p2r.at[d - 1], rowdev(yy, x)))
        p2.append(remote(pb.at[r16(xx)], r2b.at[d - 1], p2s.at[d + 2], p2r.at[d + 2], rowdev(y, xx)))
    for cp in p2:
        cp.start()

    for d in order:
        tri_z[d - 1].wait_recv()
        tri_core[d].start()

    for cp in p2:
        cp.wait_recv()
    top[rows_a(y, x), ca] = pa[r16(y), :] + r2a[0] + r2a[1] + r2a[2]
    top[rows_b(y, x), cb] = pb[r16(x), :] + r2b[0] + r2b[1] + r2b[2]

    @pl.when(jnp.logical_not(is_root))
    def _():
        scatter[0].wait_recv()
        scatter[1].wait_recv()

    p3 = []
    for w, ref in enumerate((top, old)):
        at = ref.at[rows_a(y, x), ca]
        bt = ref.at[rows_b(y, x), cb]
        for d in (1, 3, 2):
            xx, yy = (x + d) % 4, (y + d) % 4
            n = w * 6 + d - 1
            p3.append(remote(at, at, p3s.at[n], p3r.at[n], rowdev(yy, x)))
            p3.append(remote(bt, bt, p3s.at[n + 3], p3r.at[n + 3], rowdev(y, xx)))
    for cp in p3:
        cp.start()
    for cp in p3:
        cp.wait_recv()

    p4 = []
    for w, ref in enumerate((top, old)):
        at = ref.at[r64(x), ca]
        bt = ref.at[r64(y), cb]
        for d in (1, 3, 2):
            xx, yy = (x + d) % 4, (y + d) % 4
            n = w * 6 + d - 1
            p4.append(remote(at, at, p4s.at[n], p4r.at[n], rowdev(y, xx)))
            p4.append(remote(bt, bt, p4s.at[n + 3], p4r.at[n + 3], rowdev(yy, x)))
    for cp in p4:
        cp.start()

    for d in order:
        pan_z[d - 1].wait_recv()
        pan_core[d].start()

    for d in range(8):
        tri_core[d].wait_recv()
    inv[...] = upper_inverse(tri[...])
    for d in range(8):
        pan_core[d].wait_recv()

    for m in range(ROWS // NB):
        w = exact(inv[...], pan[:, m * NB : (m + 1) * NB])
        if m == 0:
            w = jnp.where(is_root, -inv[...], w)
        w = jnp.transpose(w)
        hi = w.astype(BF16)
        w_hi[m * NB : (m + 1) * NB, :] = hi
        w_lo[m * NB : (m + 1) * NB, :] = (w - hi.astype(F32)).astype(BF16)

    for cp in p4:
        cp.wait_recv()
    for cp in p1 + p2 + p3 + p4 + pan_z + pan_core + tri_z + tri_core:
        cp.wait_send()

    @pl.when(is_root)
    def _():
        for cp in tri_bcast + scatter:
            cp.wait_send()


def exchange(pivots, matrix, panel):
    vmem = pl.BlockSpec(memory_space=pltpu.VMEM)
    dma = pltpu.SemaphoreType.DMA
    return pl.pallas_call(
        exchange_kernel,
        out_shape=(
            jax.ShapeDtypeStruct((NB, COLS), F32),
            jax.ShapeDtypeStruct((NB, COLS), F32),
            jax.ShapeDtypeStruct((ROWS, NB), BF16),
            jax.ShapeDtypeStruct((ROWS, NB), BF16),
        ),
        in_specs=[pl.BlockSpec(memory_space=pltpu.SMEM), pl.BlockSpec(memory_space=pl.ANY), vmem],
        out_specs=(vmem,) * 4,
        scratch_shapes=[
            pltpu.VMEM((ROWS, COLS), F32),
            pltpu.VMEM((NB, COLS), F32),
            pltpu.VMEM((3, 64, HALF), F32),
            pltpu.VMEM((3, 64, HALF), F32),
            pltpu.VMEM((3, 16, HALF), F32),
            pltpu.VMEM((3, 16, HALF), F32),
            pltpu.VMEM((64, HALF), F32),
            pltpu.VMEM((64, HALF), F32),
            pltpu.VMEM((NB, ROWS), F32),
            pltpu.VMEM((NB, NB), F32),
            pltpu.VMEM((NB, NB), F32),
            dma((2,)),
            dma((6,)), dma((6,)), dma((6,)), dma((6,)),
            dma((12,)), dma((12,)), dma((12,)), dma((12,)),
            dma((30,)), dma((2,)), dma((15,)), dma((1,)),
            dma((7,)), dma((7,)), dma((8,)), dma((8,)),
            dma((7,)), dma((7,)), dma((8,)), dma((8,)),
        ],
        name="exchange",
        compiler_params=pltpu.CompilerParams(
            collective_id=0, has_side_effects=True, vmem_limit_bytes=40 * 1024 * 1024
        ),
    )(pivots, matrix, panel)


TILE = 256


def update_kernel(piv, mat_hbm, top, old, w_hi, w_lo, out_hbm, mat, th, tl, at_row, at_k, count, in_sem, out_sem):
    r = lax.axis_index("row")
    tiles = ROWS // TILE

    def load(t):
        rows = pl.ds(t * TILE, TILE)
        return pltpu.make_async_copy(mat_hbm.at[rows], mat.at[rows], in_sem.at[t])

    def store(t):
        rows = pl.ds(t * TILE, TILE)
        return pltpu.make_async_copy(mat.at[rows], out_hbm.at[rows], out_sem.at[t])

    for t in range(tiles):
        load(t).start()
    first = r * ROWS
    count[0] = 0

    def collect(i, carry):
        off = piv[i] - first

        @pl.when((off >= 0) & (off < ROWS))
        def _():
            n = count[0]
            at_row[n] = off
            at_k[n] = i
            count[0] = n + 1

        return carry

    lax.fori_loop(0, NB, collect, 0)
    hi = top[...].astype(BF16)
    th[...] = hi
    tl[...] = (top[...] - hi.astype(F32)).astype(BF16)
    for t in range(tiles):
        load(t).wait()

    def place(n, carry):
        mat[pl.ds(at_row[n], 1), :] = old[pl.ds(at_k[n], 1), :]
        return carry

    lax.fori_loop(0, count[0], place, 0)

    @pl.when(r == 0)
    def _():
        mat[:NB, :] = jnp.zeros((NB, COLS), F32)

    def dot(a, b):
        return jnp.dot(a, b, preferred_element_type=F32)

    for t in range(tiles):
        rows = pl.ds(t * TILE, TILE)
        a, b = w_hi[rows, :], w_lo[rows, :]
        mat[rows, :] = mat[rows, :] - (dot(a, th[...]) + (dot(b, th[...]) + dot(a, tl[...])))
        store(t).start()
    for t in range(tiles):
        store(t).wait()


def update(pivots, matrix, top, old, w_hi, w_lo):
    vmem = pl.BlockSpec(memory_space=pltpu.VMEM)
    smem = pl.BlockSpec(memory_space=pltpu.SMEM)
    anyspace = pl.BlockSpec(memory_space=pl.ANY)
    return pl.pallas_call(
        update_kernel,
        out_shape=jax.ShapeDtypeStruct((ROWS, COLS), F32),
        in_specs=[smem, anyspace, vmem, vmem, vmem, vmem],
        out_specs=anyspace,
        scratch_shapes=[
            pltpu.VMEM((ROWS, COLS), F32),
            pltpu.VMEM((NB, COLS), BF16),
            pltpu.VMEM((NB, COLS), BF16),
            pltpu.SMEM((NB,), jnp.int32),
            pltpu.SMEM((NB,), jnp.int32),
            pltpu.SMEM((1,), jnp.int32),
            pltpu.SemaphoreType.DMA((6,)),
            pltpu.SemaphoreType.DMA((6,)),
        ],
        name="update",
        compiler_params=pltpu.CompilerParams(vmem_limit_bytes=32 * 1024 * 1024),
    )(pivots, matrix, top, old, w_hi, w_lo)


def body(matrix, lower_panel, pivots):
    top, old, w_hi, w_lo = exchange(pivots, matrix, lower_panel)
    return update(pivots, matrix, top, old, w_hi, w_lo)


def solution(mesh):
    placed = (P("row", "col"), P("col", "row"), P())
    return jax.shard_map(
        body, mesh=mesh, in_specs=placed, out_specs=P("row", "col"), check_vma=False
    )
```

```python
import functools

import jax
import jax.numpy as jnp
from jax import lax
from jax.experimental import pallas as pl
from jax.experimental.pallas import tpu as pltpu
from jax.sharding import PartitionSpec as P

NB = 256
ROWS = 1536
COLS = 1024
HALF = 512
MESH = pl.DeviceIdType.MESH
F32 = jnp.float32
BF16 = jnp.bfloat16


def exact(a, b):
    return jnp.dot(a, b, preferred_element_type=F32, precision=lax.Precision.HIGHEST)


def inverse_stages(tri, power, inv):
    i = lax.broadcasted_iota(jnp.int32, (NB, NB), 0)
    j = lax.broadcasted_iota(jnp.int32, (NB, NB), 1)
    eye = jnp.where(i == j, 1.0, 0.0).astype(F32)

    def begin():
        power[...] = jnp.where((j > i) & (i // 32 == j // 32), tri[...], 0.0)
        inv[...] = eye - power[...]

    def square():
        squared = exact(power[...], power[...])
        power[...] = squared
        inv[...] = exact(inv[...], eye + squared)

    def double(size):
        block = (i // (2 * size) == j // (2 * size)) & (i // size < j // size)
        inv[...] = inv[...] - exact(exact(inv[...], jnp.where(block, tri[...], 0.0)), inv[...])

    steps = [begin, square, square, square, square]
    return steps + [functools.partial(double, size) for size in (32, 64, 128)]


SUB = 2
WIDE = HALF // SUB


def exchange_kernel(
    piv_hbm, mat_hbm, panel_hbm, mat, mix, top_hi, top_lo, w_hi, w_lo,
    piv, owner, sel, r1a, r1b, r2a, r2b, pa, pb, ga, gb, sa, sb, both_a, both_b, m4a, m4b, pan, tri, power, inv,
    in_sem, p1s, p1r, p2s, p2r, p3s, p3r, p4s, p4r, tbs, tbr,
    tzs, tzr, tcs, tcr, pzs, pzr, pcs, pcr,
):
    r = lax.axis_index("row")
    c = lax.axis_index("col")
    y, x = r // 4, r % 4
    z, k = c // 2, c % 2
    is_root = r == 0

    def piece(ref, zz, kk):
        return ref.at[pl.ds(pl.multiple_of((zz * 2 + kk) * 16, 16), 16)]

    my_pan = piece(pan, z, k)
    my_tri = piece(tri, z, k)
    load_pan = pltpu.make_async_copy(panel_hbm, my_pan, in_sem.at[0])
    load_piv = pltpu.make_async_copy(piv_hbm, piv, in_sem.at[1])
    load_mat = pltpu.make_async_copy(mat_hbm, mat, in_sem.at[2])
    load_pan.start()
    load_piv.start()
    load_mat.start()

    def rowdev(yy, xx):
        return (yy * 4 + xx, c)

    def coldev(zz, kk):
        return (r, zz * 2 + kk)

    barrier = pltpu.get_barrier_semaphore()
    for d in range(1, 4):
        pl.semaphore_signal(barrier, inc=1, device_id=rowdev(y, (x + d) % 4), device_id_type=MESH)
        pl.semaphore_signal(barrier, inc=1, device_id=rowdev((y + d) % 4, x), device_id_type=MESH)
    for d in range(1, 8):
        pl.semaphore_signal(barrier, inc=1, device_id=coldev((z + d) % 8, k), device_id_type=MESH)
    pl.semaphore_signal(barrier, inc=1, device_id=coldev(z, 1 - k), device_id_type=MESH)
    pl.semaphore_wait(barrier, 14)

    def remote(src, dst, ss, rs, dev):
        return pltpu.make_async_remote_copy(
            src_ref=src, dst_ref=dst, send_sem=ss, recv_sem=rs, device_id=dev, device_id_type=MESH
        )

    def r64(i):
        return pl.ds(pl.multiple_of(i * 64, 64), 64)

    def r16(i):
        return pl.ds(pl.multiple_of(i * 16, 16), 16)

    def group(outer, inner):
        return pl.ds(pl.multiple_of(outer * 64 + inner * 16, 16), 16)

    near = (1, 3, 2)

    load_pan.wait()
    tri_x = [
        remote(my_pan.at[:, pl.ds(0, NB)], my_tri, tbs.at[d - 1], tbr.at[0], rowdev(y, (x + d) % 4)) for d in range(1, 4)
    ]
    tri_y = [remote(my_tri, my_tri, tbs.at[d + 2], tbr.at[1], rowdev((y + d) % 4, x)) for d in range(1, 4)]

    @pl.when(is_root)
    def _():
        for cp in tri_x:
            cp.start()
        mine = pl.ds(pl.multiple_of(c * 16, 16), 16)
        tri[mine, :] = pan[mine, :NB]

    def column(ref, zs, zr, cs, cr):
        mine = piece(ref, z, k)
        along = {d: remote(mine, mine, zs.at[d - 1], zr.at[d - 1], coldev((z + d) % 8, k)) for d in range(1, 8)}
        across = []
        for d in range(8):
            got = piece(ref, (z + 8 - d) % 8, k)
            across.append(remote(got, got, cs.at[d], cr.at[d], coldev(z, 1 - k)))
        return along, across

    tri_z, tri_core = column(tri, tzs, tzr, tcs, tcr)
    pan_z, pan_core = column(pan, pzs, pzr, pcs, pcr)
    early, late = (1, 7, 2, 6), (3, 5, 4)
    order = early + late
    for d in early:
        pan_z[d].start()
    pan_core[0].start()

    load_piv.wait()
    load_mat.wait()
    first = r * ROWS

    def pick(g, carry):
        for i in range(8):
            at = pl.ds(g * 8 + i, 1)
            pivot = piv[g * 8 + i]
            off = pivot - first
            own = (off >= 0) & (off < ROWS)
            row = mat[pl.ds(jnp.clip(off, 0, ROWS - 1), 1), :]
            sel[at, :] = jnp.where(own, row, jnp.where(is_root, mat[at, :], 0.0))
            owner[at, :] = jnp.full((1, WIDE), ((pivot >> 9) * 43691) >> 17, jnp.int32)
        return carry

    lax.fori_loop(0, NB // 8, pick, 0)

    def ca(s):
        return pl.ds(s * WIDE, WIDE)

    def cb(s):
        return pl.ds(HALF + s * WIDE, WIDE)

    def around(s, ss, rs, part_a, part_b, a_along_x):
        copies = []
        for d in near:
            xx, yy = (x + d) % 4, (y + d) % 4
            at, bt = s * 6 + d - 1, s * 6 + d + 2
            to_x, to_y = rowdev(y, xx), rowdev(yy, x)
            src, dst = part_a(xx if a_along_x else yy, d - 1)
            copies.append(remote(src, dst, ss.at[at], rs.at[at], to_x if a_along_x else to_y))
            src, dst = part_b(yy if a_along_x else xx, d - 1)
            copies.append(remote(src, dst, ss.at[bt], rs.at[bt], to_y if a_along_x else to_x))
        return copies

    def start(copies):
        for cp in copies:
            cp.start()

    def arrive(copies):
        for cp in copies:
            cp.wait_recv()

    p1, p2, p3, p4 = [], [], [], []
    for s in range(SUB):
        p1.append(around(
            s, p1s, p1r,
            lambda to, d: (sel.at[r64(to), ca(s)], r1a.at[s, d]),
            lambda to, d: (sel.at[r64(to), cb(s)], r1b.at[s, d]), True))
        p2.append(around(
            s, p2s, p2r,
            lambda to, d: (sa.at[s, r16(to)], r2a.at[s, d]),
            lambda to, d: (sb.at[s, r16(to)], r2b.at[s, d]), False))
        p3.append(around(
            s, p3s, p3r,
            lambda to, d: (both_a.at[s, y],) * 2,
            lambda to, d: (both_b.at[s, x],) * 2, False))
        p4.append(around(
            s, p4s, p4r,
            lambda to, d: (m4a.at[s, d], mix.at[r64(x), ca(s)]),
            lambda to, d: (m4b.at[s, d], mix.at[r64(y), cb(s)]), True))
        start(p1[s])

    def total(parts, here, foreign):
        out = None
        for i, part in enumerate(parts):
            part = jnp.where(here == i, jnp.where(foreign, 0.0, part), part)
            out = part if out is None else out + part
        return out

    def one_of(parts, here):
        out = parts[3]
        for i in (2, 1, 0):
            out = jnp.where(here == i, parts[i], out)
        return out

    def add_one(s):
        arrive(p1[s])
        for cols, along, across, got, part, group_old, send, is_line in (
            (ca(s), x, y, r1a, pa, ga, sa, lambda dev: dev >> 2),
            (cb(s), y, x, r1b, pb, gb, sb, lambda dev: dev & 3),
        ):
            dev = owner[r64(along), :]
            parts = [sel[r64(along), cols], got[s, 0], got[s, 1], got[s, 2]]
            summed = total(parts, jnp.where(across == 0, along, -1), dev != 0)
            old = one_of(parts, along)
            part[s] = summed
            group_old[s] = old
            send[s] = jnp.where(is_line(dev) == 0, summed, jnp.where(across == 0, old, summed))
        start(p2[s])

    def add_two(s):
        arrive(p2[s])
        for along, across, got, part, group_old, both, is_line in (
            (x, y, r2a, pa, ga, both_a, lambda dev: dev >> 2),
            (y, x, r2b, pb, gb, both_b, lambda dev: dev & 3),
        ):
            dev = owner[group(along, across), :]
            parts = [part[s, r16(across), :], got[s, 0], got[s, 1], got[s, 2]]
            both[s, across, 0] = total(parts, jnp.where(across == 0, -1, across), is_line(dev) != 0)
            both[s, across, 1] = one_of([group_old[s, r16(across), :], parts[1], parts[2], parts[3]], across)
        start(p3[s])

    def last(s):
        arrive(p3[s])
        for cols, along, across, both, group_old, send, number in (
            (ca(s), x, y, both_a, ga, m4a, lambda to: y * 4 + to),
            (cb(s), y, x, both_b, gb, m4b, lambda to: to * 4 + x),
        ):
            dev = owner[r64(along), :]
            new = both[s, :, 0].reshape(64, WIDE)
            old = jnp.where(across == 0, group_old[s], both[s, :, 1].reshape(64, WIDE))
            for d in near:
                send[s, d - 1] = jnp.where(dev == number((along + d) % 4), old, new)
            mix[r64(along), cols] = jnp.where(dev == r, old, new)
        start(p4[s])

    def finish(s):
        arrive(p4[s])
        for cols in (ca(s), cb(s)):
            new = jnp.where(owner[...] == r, sel[:, cols], mix[:, cols])
            hi = new.astype(BF16)
            top_hi[:, cols] = hi
            top_lo[:, cols] = (new - hi.astype(F32)).astype(BF16)

    @pl.when((y == 0) & (x != 0))
    def _():
        tri_x[0].wait_recv()

    @pl.when(y == 0)
    def _():
        for cp in tri_y:
            cp.start()

    @pl.when(y != 0)
    def _():
        tri_y[0].wait_recv()

    for d in order:
        tri_z[d].start()
    tri_core[0].start()
    for d in late:
        pan_z[d].start()

    add_one(0)
    add_one(1)
    for d in order:
        tri_z[d].wait_recv()
        tri_core[d].start()
    add_two(0)
    add_two(1)
    for d in range(8):
        tri_core[d].wait_recv()
    stages = inverse_stages(tri, power, inv)
    for stage in stages[:3]:
        stage()
    last(0)
    stages[3]()
    last(1)
    for stage in stages[4:]:
        stage()
    for d in order:
        pan_z[d].wait_recv()
        pan_core[d].start()
    for d in range(8):
        pan_core[d].wait_recv()

    for m in range(ROWS // NB):
        w = exact(inv[...], pan[:, m * NB : (m + 1) * NB])
        if m == 0:
            w = jnp.where(is_root, -inv[...], w)
        w = jnp.transpose(w)
        hi = w.astype(BF16)
        w_hi[m * NB : (m + 1) * NB, :] = hi
        w_lo[m * NB : (m + 1) * NB, :] = (w - hi.astype(F32)).astype(BF16)

    for s in range(SUB):
        finish(s)
    for copies in p1 + p2 + p3 + p4 + [pan_z.values(), pan_core, tri_z.values(), tri_core]:
        for cp in copies:
            cp.wait_send()

    @pl.when(is_root)
    def _():
        for cp in tri_x:
            cp.wait_send()

    @pl.when(y == 0)
    def _():
        for cp in tri_y:
            cp.wait_send()


def exchange(pivots, matrix, panel):
    vmem = pl.BlockSpec(memory_space=pltpu.VMEM)
    hbm = pl.BlockSpec(memory_space=pltpu.HBM)
    dma = pltpu.SemaphoreType.DMA
    return pl.pallas_call(
        exchange_kernel,
        out_shape=(
            pltpu.VMEM((ROWS, COLS), F32),
            jax.ShapeDtypeStruct((NB, COLS), F32),
            jax.ShapeDtypeStruct((NB, COLS), BF16),
            jax.ShapeDtypeStruct((NB, COLS), BF16),
            jax.ShapeDtypeStruct((ROWS, NB), BF16),
            jax.ShapeDtypeStruct((ROWS, NB), BF16),
        ),
        in_specs=[hbm, hbm, hbm],
        out_specs=(vmem,) * 6,
        scratch_shapes=[
            pltpu.SMEM((NB,), jnp.int32),
            pltpu.VMEM((NB, WIDE), jnp.int32),
            pltpu.VMEM((NB, COLS), F32),
            pltpu.VMEM((SUB, 3, 64, WIDE), F32),
            pltpu.VMEM((SUB, 3, 64, WIDE), F32),
            pltpu.VMEM((SUB, 3, 16, WIDE), F32),
            pltpu.VMEM((SUB, 3, 16, WIDE), F32),
            pltpu.VMEM((SUB, 64, WIDE), F32),
            pltpu.VMEM((SUB, 64, WIDE), F32),
            pltpu.VMEM((SUB, 64, WIDE), F32),
            pltpu.VMEM((SUB, 64, WIDE), F32),
            pltpu.VMEM((SUB, 64, WIDE), F32),
            pltpu.VMEM((SUB, 64, WIDE), F32),
            pltpu.VMEM((SUB, 4, 2, 16, WIDE), F32),
            pltpu.VMEM((SUB, 4, 2, 16, WIDE), F32),
            pltpu.VMEM((SUB, 3, 64, WIDE), F32),
            pltpu.VMEM((SUB, 3, 64, WIDE), F32),
            pltpu.VMEM((NB, ROWS), F32),
            pltpu.VMEM((NB, NB), F32),
            pltpu.VMEM((NB, NB), F32),
            pltpu.VMEM((NB, NB), F32),
            dma((3,)),
            dma((6 * SUB,)), dma((6 * SUB,)), dma((6 * SUB,)), dma((6 * SUB,)),
            dma((6 * SUB,)), dma((6 * SUB,)), dma((6 * SUB,)), dma((6 * SUB,)),
            dma((6,)), dma((2,)),
            dma((7,)), dma((7,)), dma((8,)), dma((8,)),
            dma((7,)), dma((7,)), dma((8,)), dma((8,)),
        ],
        name="exchange",
        compiler_params=pltpu.CompilerParams(
            collective_id=0, has_side_effects=True, vmem_limit_bytes=24 * 1024 * 1024
        ),
    )(*(pltpu.with_memory_space_constraint(a, pltpu.HBM) for a in (pivots, matrix, panel)))


TILE = 256


def update_kernel(piv, mat, mix, th, tl, w_hi, w_lo, out_hbm, out, at_row, at_k, out_sem):
    r = lax.axis_index("row")
    tiles = ROWS // TILE

    def store(t):
        rows = pl.ds(t * TILE, TILE)
        return pltpu.make_async_copy(out.at[rows], out_hbm.at[rows], out_sem.at[t])

    first = r * ROWS

    def collect(g, n):
        for i in range(8):
            off = piv[g * 8 + i] - first
            at_row[n] = off
            at_k[n] = g * 8 + i
            n = n + jnp.where((off >= 0) & (off < ROWS), 1, 0)
        return n

    count = lax.fori_loop(0, NB // 8, collect, 0)

    def dot(a, b):
        return jnp.dot(a, b, preferred_element_type=F32)

    for t in range(tiles):
        rows = pl.ds(t * TILE, TILE)
        a, b = w_hi[rows, :], w_lo[rows, :]
        base = mat[rows, :]
        if t == 0:
            base = jnp.where(r == 0, 0.0, base)
        out[rows, :] = base - (dot(a, th[...]) + (dot(b, th[...]) + dot(a, tl[...])))

        def fix(n, carry):
            row = at_row[n]

            @pl.when((row >= t * TILE) & (row < (t + 1) * TILE))
            def _():
                one = pl.ds(row, 1)
                k = pl.ds(at_k[n], 1)
                old = jnp.where(r == 0, mat[k, :], mix[k, :])
                out[one, :] = out[one, :] + (old - mat[one, :])

            return carry

        lax.fori_loop(0, count, fix, 0)
        store(t).start()
    for t in range(tiles):
        store(t).wait()


def update(pivots, matrix, mix, top_hi, top_lo, w_hi, w_lo):
    vmem = pl.BlockSpec(memory_space=pltpu.VMEM)
    smem = pl.BlockSpec(memory_space=pltpu.SMEM)
    return pl.pallas_call(
        update_kernel,
        out_shape=jax.ShapeDtypeStruct((ROWS, COLS), F32),
        in_specs=[smem] + [vmem] * 6,
        out_specs=pl.BlockSpec(memory_space=pl.ANY),
        scratch_shapes=[
            pltpu.VMEM((ROWS, COLS), F32),
            pltpu.SMEM((NB + 8,), jnp.int32),
            pltpu.SMEM((NB + 8,), jnp.int32),
            pltpu.SemaphoreType.DMA((6,)),
        ],
        name="update",
        compiler_params=pltpu.CompilerParams(vmem_limit_bytes=24 * 1024 * 1024),
    )(pivots, matrix, mix, top_hi, top_lo, w_hi, w_lo)


def body(matrix, lower_panel, pivots):
    return update(pivots, *exchange(pivots, matrix, lower_panel))


def solution(mesh):
    placed = (P("row", "col"), P("col", "row"), P())
    return jax.shard_map(
        body, mesh=mesh, in_specs=placed, out_specs=P("row", "col"), check_vma=False
    )
```

```python
import functools

import jax
import jax.numpy as jnp
from jax import lax
from jax.experimental import pallas as pl
from jax.experimental.pallas import tpu as pltpu
from jax.sharding import PartitionSpec as P

NB = 256
ROWS = 1536
COLS = 1024
HALF = 512
MESH = pl.DeviceIdType.MESH
F32 = jnp.float32
BF16 = jnp.bfloat16


def exact(a, b):
    return jnp.dot(a, b, preferred_element_type=F32, precision=lax.Precision.HIGHEST)


def inverse_stages(tri, power, inv):
    i = lax.broadcasted_iota(jnp.int32, (NB, NB), 0)
    j = lax.broadcasted_iota(jnp.int32, (NB, NB), 1)
    eye = jnp.where(i == j, 1.0, 0.0).astype(F32)

    def begin():
        power[...] = jnp.where((j > i) & (i // 32 == j // 32), tri[...], 0.0)
        inv[...] = eye - power[...]

    def square():
        squared = exact(power[...], power[...])
        power[...] = squared
        inv[...] = exact(inv[...], eye + squared)

    def double(size):
        block = (i // (2 * size) == j // (2 * size)) & (i // size < j // size)
        inv[...] = inv[...] - exact(exact(inv[...], jnp.where(block, tri[...], 0.0)), inv[...])

    steps = [begin, square, square, square, square]
    return steps + [functools.partial(double, size) for size in (32, 64, 128)]


SUB = 2
TILE = 256
TILES = ROWS // TILE
WIDE = HALF // SUB


def exchange_kernel(
    piv_hbm, mat_hbm, panel_hbm, mat, lists, mix, top_hi, top_lo, w_hi, w_lo,
    piv, column_of, owner, sel, r1a, r1b, r2a, r2b, pa, pb, ga, gb, sa, sb, both_a, both_b, m4a, m4b, pan, tri, power, inv,
    in_sem, p1s, p1r, p2s, p2r, p3s, p3r, p4s, p4r, tbs, tbr,
    tzs, tzr, tcs, tcr, pzs, pzr, pcs, pcr,
):
    r = lax.axis_index("row")
    c = lax.axis_index("col")
    y, x = r // 4, r % 4
    z, k = c // 2, c % 2
    is_root = r == 0

    def piece(ref, zz, kk):
        return ref.at[pl.ds(pl.multiple_of((zz * 2 + kk) * 16, 16), 16)]

    my_pan = piece(pan, z, k)
    my_tri = piece(tri, z, k)
    load_pan = pltpu.make_async_copy(panel_hbm, my_pan, in_sem.at[0])
    load_piv = pltpu.make_async_copy(piv_hbm, piv, in_sem.at[1])
    load_mat = pltpu.make_async_copy(mat_hbm, mat, in_sem.at[2])
    load_pan.start()
    load_piv.start()
    load_mat.start()

    def rowdev(yy, xx):
        return (yy * 4 + xx, c)

    def coldev(zz, kk):
        return (r, zz * 2 + kk)

    barrier = pltpu.get_barrier_semaphore()
    for d in range(1, 4):
        pl.semaphore_signal(barrier, inc=1, device_id=rowdev(y, (x + d) % 4), device_id_type=MESH)
        pl.semaphore_signal(barrier, inc=1, device_id=rowdev((y + d) % 4, x), device_id_type=MESH)
    for d in range(1, 8):
        pl.semaphore_signal(barrier, inc=1, device_id=coldev((z + d) % 8, k), device_id_type=MESH)
    pl.semaphore_signal(barrier, inc=1, device_id=coldev(z, 1 - k), device_id_type=MESH)


    load_piv.wait()
    load_mat.wait()
    first = r * ROWS

    def pick(g, carry):
        for i in range(8):
            at = pl.ds(g * 8 + i, 1)
            pivot = piv[g * 8 + i]
            off = pivot - first
            own = (off >= 0) & (off < ROWS)
            row = mat[pl.ds(jnp.clip(off, 0, ROWS - 1), 1), :]
            sel[at, :] = jnp.where(own, row, jnp.where(is_root, mat[at, :], 0.0))
            column_of[at, :] = jnp.full((1, WIDE), pivot, jnp.int32)
        return carry

    lax.fori_loop(0, NB // 16, pick, 0)
    pl.semaphore_wait(barrier, 14)

    def remote(src, dst, ss, rs, dev):
        return pltpu.make_async_remote_copy(
            src_ref=src, dst_ref=dst, send_sem=ss, recv_sem=rs, device_id=dev, device_id_type=MESH
        )

    def r64(i):
        return pl.ds(pl.multiple_of(i * 64, 64), 64)

    def r16(i):
        return pl.ds(pl.multiple_of(i * 16, 16), 16)

    def group(outer, inner):
        return pl.ds(pl.multiple_of(outer * 64 + inner * 16, 16), 16)

    near = (1, 3, 2)

    load_pan.wait()
    tri_x = [
        remote(my_pan.at[:, pl.ds(0, NB)], my_tri, tbs.at[d - 1], tbr.at[0], rowdev(y, (x + d) % 4)) for d in range(1, 4)
    ]
    tri_y = [remote(my_tri, my_tri, tbs.at[d + 2], tbr.at[1], rowdev((y + d) % 4, x)) for d in range(1, 4)]

    @pl.when(is_root)
    def _():
        for cp in tri_x:
            cp.start()
        mine = pl.ds(pl.multiple_of(c * 16, 16), 16)
        tri[mine, :] = pan[mine, :NB]

    def column(ref, zs, zr, cs, cr):
        mine = piece(ref, z, k)
        along = {d: remote(mine, mine, zs.at[d - 1], zr.at[d - 1], coldev((z + d) % 8, k)) for d in range(1, 8)}
        across = []
        for d in range(8):
            got = piece(ref, (z + 8 - d) % 8, k)
            across.append(remote(got, got, cs.at[d], cr.at[d], coldev(z, 1 - k)))
        return along, across

    tri_z, tri_core = column(tri, tzs, tzr, tcs, tcr)
    pan_z, pan_core = column(pan, pzs, pzr, pcs, pcr)
    early = (1, 7, 2, 6)
    order = early + (3, 5, 4)
    for d, held, step in ((3, 2, 1), (5, 6, 7), (4, 2, 2)):
        got = piece(pan, (z + 8 - held) % 8, k)
        pan_z[d] = remote(got, got, pzs.at[d - 1], pzr.at[d - 1], coldev((z + step) % 8, k))
    for d in early:
        pan_z[d].start()
    pan_core[0].start()

    lax.fori_loop(NB // 16, NB // 8, pick, 0)
    owner[...] = ((column_of[...] >> 9) * 43691) >> 17

    @pl.when((y == 0) & (x != 0))
    def _():
        tri_x[0].wait_recv()

    @pl.when(y == 0)
    def _():
        for cp in tri_y:
            cp.start()

    def ca(s):
        return pl.ds(s * WIDE, WIDE)

    def cb(s):
        return pl.ds(HALF + s * WIDE, WIDE)

    def around(s, ss, rs, part_a, part_b, a_along_x):
        copies = []
        for d in near:
            xx, yy = (x + d) % 4, (y + d) % 4
            at, bt = s * 6 + d - 1, s * 6 + d + 2
            to_x, to_y = rowdev(y, xx), rowdev(yy, x)
            src, dst = part_a(xx if a_along_x else yy, d - 1)
            copies.append(remote(src, dst, ss.at[at], rs.at[at], to_x if a_along_x else to_y))
            src, dst = part_b(yy if a_along_x else xx, d - 1)
            copies.append(remote(src, dst, ss.at[bt], rs.at[bt], to_y if a_along_x else to_x))
        return copies

    def start(copies):
        for cp in copies:
            cp.start()

    def arrive(copies):
        for cp in copies:
            cp.wait_recv()

    p1, p2, p3, p4 = [], [], [], []
    for s in range(SUB):
        p1.append(around(
            s, p1s, p1r,
            lambda to, d: (sel.at[r64(to), ca(s)], r1a.at[s, d]),
            lambda to, d: (sel.at[r64(to), cb(s)], r1b.at[s, d]), True))
        p2.append(around(
            s, p2s, p2r,
            lambda to, d: (sa.at[s, r16(to)], r2a.at[s, d]),
            lambda to, d: (sb.at[s, r16(to)], r2b.at[s, d]), False))
        p3.append(around(
            s, p3s, p3r,
            lambda to, d: (both_a.at[s, y],) * 2,
            lambda to, d: (both_b.at[s, x],) * 2, False))
        p4.append(around(
            s, p4s, p4r,
            lambda to, d: (m4a.at[s, d], mix.at[r64(x), ca(s)]),
            lambda to, d: (m4b.at[s, d], mix.at[r64(y), cb(s)]), True))
        start(p1[s])

    def total(parts, here, foreign):
        out = None
        for i, part in enumerate(parts):
            part = jnp.where(here == i, jnp.where(foreign, 0.0, part), part)
            out = part if out is None else out + part
        return out

    def one_of(parts, here):
        out = parts[3]
        for i in (2, 1, 0):
            out = jnp.where(here == i, parts[i], out)
        return out

    def add_one(s):
        arrive(p1[s])
        for cols, along, across, got, part, group_old, send, is_line in (
            (ca(s), x, y, r1a, pa, ga, sa, lambda dev: dev >> 2),
            (cb(s), y, x, r1b, pb, gb, sb, lambda dev: dev & 3),
        ):
            dev = owner[r64(along), :]
            parts = [sel[r64(along), cols], got[s, 0], got[s, 1], got[s, 2]]
            summed = total(parts, jnp.where(across == 0, along, -1), dev != 0)
            old = one_of(parts, along)
            part[s] = summed
            group_old[s] = old
            send[s] = jnp.where(is_line(dev) == 0, summed, jnp.where(across == 0, old, summed))
        start(p2[s])

    def add_two(s):
        arrive(p2[s])
        for along, across, got, part, group_old, both, is_line in (
            (x, y, r2a, pa, ga, both_a, lambda dev: dev >> 2),
            (y, x, r2b, pb, gb, both_b, lambda dev: dev & 3),
        ):
            dev = owner[group(along, across), :]
            parts = [part[s, r16(across), :], got[s, 0], got[s, 1], got[s, 2]]
            both[s, across, 0] = total(parts, jnp.where(across == 0, -1, across), is_line(dev) != 0)
            both[s, across, 1] = one_of([group_old[s, r16(across), :], parts[1], parts[2], parts[3]], across)
        start(p3[s])

    def last(s):
        arrive(p3[s])
        for cols, along, across, both, group_old, send, number in (
            (ca(s), x, y, both_a, ga, m4a, lambda to: y * 4 + to),
            (cb(s), y, x, both_b, gb, m4b, lambda to: to * 4 + x),
        ):
            dev = owner[r64(along), :]
            new = both[s, :, 0].reshape(64, WIDE)
            old = jnp.where(across == 0, group_old[s], both[s, :, 1].reshape(64, WIDE))
            for d in near:
                send[s, d - 1] = jnp.where(dev == number((along + d) % 4), old, new)
            mix[r64(along), cols] = jnp.where(dev == r, old, new)
        start(p4[s])

    def finish(s):
        arrive(p4[s])
        for cols in (ca(s), cb(s)):
            new = jnp.where(owner[...] == r, sel[:, cols], mix[:, cols])
            hi = new.astype(BF16)
            top_hi[:, cols] = hi
            top_lo[:, cols] = (new - hi.astype(F32)).astype(BF16)

    @pl.when(y != 0)
    def _():
        tri_y[0].wait_recv()

    for d in order:
        tri_z[d].start()
    tri_core[0].start()
    for d in (2, 6):
        pan_z[d].wait_recv()
        pan_core[d].start()
    for d in (3, 5, 4):
        pan_z[d].start()

    local = column_of[...] - first
    number = lax.broadcasted_iota(jnp.int32, (NB, NB), 0)
    slot = lax.broadcasted_iota(jnp.int32, (NB, NB), 1)
    before = jnp.where(number > slot, 1.0, 0.0).astype(BF16)
    lists[...] = jnp.zeros_like(lists)
    for t in range(TILES):
        inside = (local >= t * TILE) & (local < (t + 1) * TILE)
        rank = jnp.dot(before, jnp.where(inside, 1.0, 0.0).astype(BF16), preferred_element_type=F32)
        packed = jnp.where(inside & (rank.astype(jnp.int32) == slot), local * NB + number, 0)
        lists[t : t + 1, :] = jnp.sum(packed, axis=0, keepdims=True)
        lists[8 + t : 9 + t, :] = jnp.sum(jnp.where(inside, 1, 0), axis=0, keepdims=True)

    add_one(0)
    for d in order:
        tri_z[d].wait_recv()
        tri_core[d].start()
    add_one(1)
    add_two(0)
    add_two(1)
    for d in range(8):
        tri_core[d].wait_recv()
    stages = inverse_stages(tri, power, inv)
    for stage in stages[:3]:
        stage()
    last(0)
    stages[3]()
    last(1)
    for stage in stages[4:]:
        stage()
    for d in (1, 7, 3, 5, 4):
        pan_z[d].wait_recv()
        pan_core[d].start()
    for d in range(8):
        pan_core[d].wait_recv()

    for m in range(ROWS // NB):
        w = exact(inv[...], pan[:, m * NB : (m + 1) * NB])
        if m == 0:
            w = jnp.where(is_root, -inv[...], w)
        w = jnp.transpose(w)
        hi = w.astype(BF16)
        w_hi[m * NB : (m + 1) * NB, :] = hi
        w_lo[m * NB : (m + 1) * NB, :] = (w - hi.astype(F32)).astype(BF16)

    for s in range(SUB):
        finish(s)
    for copies in p1 + p2 + p3 + p4 + [pan_z.values(), pan_core, tri_z.values(), tri_core]:
        for cp in copies:
            cp.wait_send()

    @pl.when(is_root)
    def _():
        for cp in tri_x:
            cp.wait_send()

    @pl.when(y == 0)
    def _():
        for cp in tri_y:
            cp.wait_send()


def exchange(pivots, matrix, panel):
    vmem = pl.BlockSpec(memory_space=pltpu.VMEM)
    hbm = pl.BlockSpec(memory_space=pltpu.HBM)
    dma = pltpu.SemaphoreType.DMA
    return pl.pallas_call(
        exchange_kernel,
        out_shape=(
            pltpu.VMEM((ROWS, COLS), F32),
            jax.ShapeDtypeStruct((16, NB), jnp.int32),
            jax.ShapeDtypeStruct((NB, COLS), F32),
            jax.ShapeDtypeStruct((NB, COLS), BF16),
            jax.ShapeDtypeStruct((NB, COLS), BF16),
            jax.ShapeDtypeStruct((ROWS, NB), BF16),
            jax.ShapeDtypeStruct((ROWS, NB), BF16),
        ),
        in_specs=[hbm, hbm, hbm],
        out_specs=(vmem,) * 7,
        scratch_shapes=[
            pltpu.SMEM((NB,), jnp.int32),
            pltpu.VMEM((NB, WIDE), jnp.int32),
            pltpu.VMEM((NB, WIDE), jnp.int32),
            pltpu.VMEM((NB, COLS), F32),
            pltpu.VMEM((SUB, 3, 64, WIDE), F32),
            pltpu.VMEM((SUB, 3, 64, WIDE), F32),
            pltpu.VMEM((SUB, 3, 16, WIDE), F32),
            pltpu.VMEM((SUB, 3, 16, WIDE), F32),
            pltpu.VMEM((SUB, 64, WIDE), F32),
            pltpu.VMEM((SUB, 64, WIDE), F32),
            pltpu.VMEM((SUB, 64, WIDE), F32),
            pltpu.VMEM((SUB, 64, WIDE), F32),
            pltpu.VMEM((SUB, 64, WIDE), F32),
            pltpu.VMEM((SUB, 64, WIDE), F32),
            pltpu.VMEM((SUB, 4, 2, 16, WIDE), F32),
            pltpu.VMEM((SUB, 4, 2, 16, WIDE), F32),
            pltpu.VMEM((SUB, 3, 64, WIDE), F32),
            pltpu.VMEM((SUB, 3, 64, WIDE), F32),
            pltpu.VMEM((NB, ROWS), F32),
            pltpu.VMEM((NB, NB), F32),
            pltpu.VMEM((NB, NB), F32),
            pltpu.VMEM((NB, NB), F32),
            dma((3,)),
            dma((6 * SUB,)), dma((6 * SUB,)), dma((6 * SUB,)), dma((6 * SUB,)),
            dma((6 * SUB,)), dma((6 * SUB,)), dma((6 * SUB,)), dma((6 * SUB,)),
            dma((6,)), dma((2,)),
            dma((7,)), dma((7,)), dma((8,)), dma((8,)),
            dma((7,)), dma((7,)), dma((8,)), dma((8,)),
        ],
        name="exchange",
        compiler_params=pltpu.CompilerParams(
            collective_id=0, has_side_effects=True, vmem_limit_bytes=24 * 1024 * 1024
        ),
    )(*(pltpu.with_memory_space_constraint(a, pltpu.HBM) for a in (pivots, matrix, panel)))


def update_kernel(mat, lists, mix, th, tl, w_hi, w_lo, out_hbm, out, swaps, list_sem, out_sem):
    r = lax.axis_index("row")
    load = pltpu.make_async_copy(lists, swaps, list_sem)
    load.start()

    def store(t):
        rows = pl.ds(t * TILE, TILE)
        return pltpu.make_async_copy(out.at[rows], out_hbm.at[rows], out_sem.at[t])

    def dot(a, b):
        return jnp.dot(a, b, preferred_element_type=F32)

    for t in range(TILES):
        rows = pl.ds(t * TILE, TILE)
        a, b = w_hi[rows, :], w_lo[rows, :]
        base = mat[rows, :]
        if t == 0:
            base = jnp.where(r == 0, 0.0, base)
        out[rows, :] = base - (dot(a, th[...]) + (dot(b, th[...]) + dot(a, tl[...])))
        if t == 0:
            load.wait()

        def fix(n, carry):
            entry = swaps[t, n]
            one, k = pl.ds(entry >> 8, 1), pl.ds(entry & (NB - 1), 1)
            old = jnp.where(r == 0, mat[k, :], mix[k, :])
            out[one, :] = out[one, :] + (old - mat[one, :])
            return carry

        lax.fori_loop(0, swaps[8 + t, 0], fix, 0)
        store(t).start()
    for t in range(TILES):
        store(t).wait()


def update(matrix, lists, mix, top_hi, top_lo, w_hi, w_lo):
    vmem = pl.BlockSpec(memory_space=pltpu.VMEM)
    anyspace = pl.BlockSpec(memory_space=pl.ANY)
    return pl.pallas_call(
        update_kernel,
        out_shape=jax.ShapeDtypeStruct((ROWS, COLS), F32),
        in_specs=[vmem, anyspace] + [vmem] * 5,
        out_specs=anyspace,
        scratch_shapes=[
            pltpu.VMEM((ROWS, COLS), F32),
            pltpu.SMEM((16, NB), jnp.int32),
            pltpu.SemaphoreType.DMA,
            pltpu.SemaphoreType.DMA((TILES,)),
        ],
        name="update",
        compiler_params=pltpu.CompilerParams(vmem_limit_bytes=24 * 1024 * 1024),
    )(matrix, lists, mix, top_hi, top_lo, w_hi, w_lo)


def body(matrix, lower_panel, pivots):
    return update(*exchange(pivots, matrix, lower_panel))


def solution(mesh):
    placed = (P("row", "col"), P("col", "row"), P())
    return jax.shard_map(
        body, mesh=mesh, in_specs=placed, out_specs=P("row", "col"), check_vma=False
    )
```

```python
import functools

import jax
import jax.numpy as jnp
from jax import lax
from jax.experimental import pallas as pl
from jax.experimental.pallas import tpu as pltpu
from jax.sharding import PartitionSpec as P

NB = 256
ROWS = 1536
COLS = 1024
HALF = 512
MESH = pl.DeviceIdType.MESH
F32 = jnp.float32
BF16 = jnp.bfloat16


def exact(a, b):
    return jnp.dot(a, b, preferred_element_type=F32, precision=lax.Precision.HIGHEST)


def three_pass(a_hi, a_lo, b_hi, b_lo):
    def dot(a, b):
        return jnp.dot(a, b, preferred_element_type=F32)

    return dot(a_hi, b_hi) + (dot(a_lo, b_hi) + dot(a_hi, b_lo))


def inverse_stages(tri, power, inv):
    i = lax.broadcasted_iota(jnp.int32, (NB, NB), 0)
    j = lax.broadcasted_iota(jnp.int32, (NB, NB), 1)
    eye = jnp.where(i == j, 1.0, 0.0).astype(F32)

    def begin():
        power[...] = jnp.where((j > i) & (i // 32 == j // 32), tri[...], 0.0)
        inv[...] = eye - power[...]

    def square():
        squared = exact(power[...], power[...])
        power[...] = squared
        inv[...] = exact(inv[...], eye + squared)

    def double(size):
        block = (i // (2 * size) == j // (2 * size)) & (i // size < j // size)
        inv[...] = inv[...] - exact(exact(inv[...], jnp.where(block, tri[...], 0.0)), inv[...])

    steps = [begin, square, square, square, square]
    return steps + [functools.partial(double, size) for size in (32, 64, 128)]


SUB = 2
TILE = 256
TILES = ROWS // TILE
WIDE = HALF // SUB


def exchange_kernel(
    piv_hbm, mat_hbm, panel_hbm, mat, lists, product, mix, top_hi, top_lo, w_hi, w_lo,
    piv, column_of, owner, sel, r1a, r1b, r2a, r2b, pa, pb, ga, gb, sa, sb, both_a, both_b, m4a, m4b, pan, tri, power, inv,
    in_sem, p1s, p1r, p2s, p2r, p3s, p3r, p4s, p4r, tbs, tbr,
    tzs, tzr, tcs, tcr, pzs, pzr, pcs, pcr,
):
    r = lax.axis_index("row")
    c = lax.axis_index("col")
    y, x = r // 4, r % 4
    z, k = c // 2, c % 2
    is_root = r == 0

    def piece(ref, zz, kk):
        return ref.at[pl.ds(pl.multiple_of((zz * 2 + kk) * 16, 16), 16)]

    my_pan = piece(pan, z, k)
    my_tri = piece(tri, z, k)
    load_pan = pltpu.make_async_copy(panel_hbm, my_pan, in_sem.at[0])
    load_piv = pltpu.make_async_copy(piv_hbm, piv, in_sem.at[1])
    load_mat = pltpu.make_async_copy(mat_hbm, mat, in_sem.at[2])
    load_pan.start()
    load_piv.start()
    load_mat.start()

    def rowdev(yy, xx):
        return (yy * 4 + xx, c)

    def coldev(zz, kk):
        return (r, zz * 2 + kk)

    barrier = pltpu.get_barrier_semaphore()
    for d in range(1, 4):
        pl.semaphore_signal(barrier, inc=1, device_id=rowdev(y, (x + d) % 4), device_id_type=MESH)
        pl.semaphore_signal(barrier, inc=1, device_id=rowdev((y + d) % 4, x), device_id_type=MESH)
    for d in range(1, 8):
        pl.semaphore_signal(barrier, inc=1, device_id=coldev((z + d) % 8, k), device_id_type=MESH)
    pl.semaphore_signal(barrier, inc=1, device_id=coldev(z, 1 - k), device_id_type=MESH)

    @pl.when((x != 0) & (y != 0))
    def _():
        pl.semaphore_signal(barrier, inc=1, device_id=(0, c), device_id_type=MESH)


    load_piv.wait()
    load_mat.wait()
    first = r * ROWS

    def pick(g, carry):
        for i in range(8):
            at = pl.ds(g * 8 + i, 1)
            pivot = piv[g * 8 + i]
            off = pivot - first
            own = (off >= 0) & (off < ROWS)
            row = mat[pl.ds(jnp.clip(off, 0, ROWS - 1), 1), :]
            sel[at, :] = jnp.where(own, row, jnp.where(is_root, mat[at, :], 0.0))
            column_of[at, :] = jnp.full((1, WIDE), pivot, jnp.int32)
        return carry

    lax.fori_loop(0, NB // 16, pick, 0)
    pl.semaphore_wait(barrier, jnp.where(is_root, 23, 14))

    def remote(src, dst, ss, rs, dev):
        return pltpu.make_async_remote_copy(
            src_ref=src, dst_ref=dst, send_sem=ss, recv_sem=rs, device_id=dev, device_id_type=MESH
        )

    def r64(i):
        return pl.ds(pl.multiple_of(i * 64, 64), 64)

    def r16(i):
        return pl.ds(pl.multiple_of(i * 16, 16), 16)

    def group(outer, inner):
        return pl.ds(pl.multiple_of(outer * 64 + inner * 16, 16), 16)

    near = (1, 3, 2)

    load_pan.wait()
    tri_all = [
        remote(my_pan.at[:, pl.ds(0, NB)], my_tri, tbs.at[d - 1], tbr.at[0], ((r + d) % 16, c)) for d in range(1, 16)
    ]

    @pl.when(is_root)
    def _():
        for cp in tri_all:
            cp.start()
        mine = pl.ds(pl.multiple_of(c * 16, 16), 16)
        tri[mine, :] = pan[mine, :NB]

    def column(ref, zs, zr, cs, cr):
        mine = piece(ref, z, k)
        along = {d: remote(mine, mine, zs.at[d - 1], zr.at[d - 1], coldev((z + d) % 8, k)) for d in range(1, 8)}
        across = []
        for d in range(8):
            got = piece(ref, (z + 8 - d) % 8, k)
            across.append(remote(got, got, cs.at[d], cr.at[d], coldev(z, 1 - k)))
        return along, across

    tri_z, tri_core = column(tri, tzs, tzr, tcs, tcr)
    pan_z, pan_core = column(pan, pzs, pzr, pcs, pcr)
    order = (1, 7, 2, 6, 3, 5, 4)
    for d, held, step in ((3, 2, 1), (5, 6, 7), (4, 2, 2)):
        got = piece(pan, (z + 8 - held) % 8, k)
        pan_z[d] = remote(got, got, pzs.at[d - 1], pzr.at[d - 1], coldev((z + step) % 8, k))
    for d in (1, 7, 2, 6):
        pan_z[d].start()
    pan_core[0].start()

    lax.fori_loop(NB // 16, NB // 8, pick, 0)
    owner[...] = ((column_of[...] >> 9) * 43691) >> 17

    def ca(s):
        return pl.ds(s * WIDE, WIDE)

    def cb(s):
        return pl.ds(HALF + s * WIDE, WIDE)

    def around(s, ss, rs, part_a, part_b, a_along_x):
        copies = []
        for d in near:
            xx, yy = (x + d) % 4, (y + d) % 4
            at, bt = s * 6 + d - 1, s * 6 + d + 2
            to_x, to_y = rowdev(y, xx), rowdev(yy, x)
            src, dst = part_a(xx if a_along_x else yy, d - 1)
            copies.append(remote(src, dst, ss.at[at], rs.at[at], to_x if a_along_x else to_y))
            src, dst = part_b(yy if a_along_x else xx, d - 1)
            copies.append(remote(src, dst, ss.at[bt], rs.at[bt], to_y if a_along_x else to_x))
        return copies

    def start(copies):
        for cp in copies:
            cp.start()

    def left(groups):
        for copies in groups:
            for cp in copies:
                cp.wait_send()

    def arrive(copies):
        for cp in copies:
            cp.wait_recv()

    p1, p2, p3, p4 = [], [], [], []
    for s in range(SUB):
        p1.append(around(
            s, p1s, p1r,
            lambda to, d: (sel.at[r64(to), ca(s)], r1a.at[s, d]),
            lambda to, d: (sel.at[r64(to), cb(s)], r1b.at[s, d]), True))
        p2.append(around(
            s, p2s, p2r,
            lambda to, d: (sa.at[s, r16(to)], r2a.at[s, d]),
            lambda to, d: (sb.at[s, r16(to)], r2b.at[s, d]), False))
        p3.append(around(
            s, p3s, p3r,
            lambda to, d: (both_a.at[s, y],) * 2,
            lambda to, d: (both_b.at[s, x],) * 2, False))
        p4.append(around(
            s, p4s, p4r,
            lambda to, d: (m4a.at[s, d], mix.at[r64(x), ca(s)]),
            lambda to, d: (m4b.at[s, d], mix.at[r64(y), cb(s)]), True))

    def total(parts, here, foreign):
        out = None
        for i, part in enumerate(parts):
            part = jnp.where(here == i, jnp.where(foreign, 0.0, part), part)
            out = part if out is None else out + part
        return out

    def one_of(parts, here):
        out = parts[3]
        for i in (2, 1, 0):
            out = jnp.where(here == i, parts[i], out)
        return out

    def add_one(s):
        arrive(p1[s])
        for cols, along, across, got, part, group_old, send, is_line in (
            (ca(s), x, y, r1a, pa, ga, sa, lambda dev: dev >> 2),
            (cb(s), y, x, r1b, pb, gb, sb, lambda dev: dev & 3),
        ):
            dev = owner[r64(along), :]
            parts = [sel[r64(along), cols], got[s, 0], got[s, 1], got[s, 2]]
            summed = total(parts, jnp.where(across == 0, along, -1), dev != 0)
            old = one_of(parts, along)
            part[s] = summed
            group_old[s] = old
            send[s] = jnp.where(is_line(dev) == 0, summed, jnp.where(across == 0, old, summed))
        start(p2[s])

    def add_two(s):
        arrive(p2[s])
        for along, across, got, part, group_old, both, is_line in (
            (x, y, r2a, pa, ga, both_a, lambda dev: dev >> 2),
            (y, x, r2b, pb, gb, both_b, lambda dev: dev & 3),
        ):
            dev = owner[group(along, across), :]
            parts = [part[s, r16(across), :], got[s, 0], got[s, 1], got[s, 2]]
            both[s, across, 0] = total(parts, jnp.where(across == 0, -1, across), is_line(dev) != 0)
            both[s, across, 1] = one_of([group_old[s, r16(across), :], parts[1], parts[2], parts[3]], across)
        start(p3[s])

    def last(s):
        arrive(p3[s])
        for cols, along, across, both, group_old, send, number in (
            (ca(s), x, y, both_a, ga, m4a, lambda to: y * 4 + to),
            (cb(s), y, x, both_b, gb, m4b, lambda to: to * 4 + x),
        ):
            dev = owner[r64(along), :]
            new = both[s, :, 0].reshape(64, WIDE)
            old = jnp.where(across == 0, group_old[s], both[s, :, 1].reshape(64, WIDE))
            for d in near:
                send[s, d - 1] = jnp.where(dev == number((along + d) % 4), old, new)
            mix[r64(along), cols] = jnp.where(dev == r, old, new)
        start(p4[s])

    def finish(s):
        arrive(p4[s])
        for cols in (ca(s), cb(s)):
            new = jnp.where(owner[...] == r, sel[:, cols], mix[:, cols])
            hi = new.astype(BF16)
            top_hi[:, cols] = hi
            top_lo[:, cols] = (new - hi.astype(F32)).astype(BF16)

    start(p1[0])
    start(p1[1])

    @pl.when(r != 0)
    def _():
        tri_all[0].wait_recv()

    for d in order:
        tri_z[d].start()
    tri_core[0].start()
    local = column_of[...] - first
    number = lax.broadcasted_iota(jnp.int32, (NB, NB), 0)
    slot = lax.broadcasted_iota(jnp.int32, (NB, NB), 1)
    before = jnp.where(number > slot, 1.0, 0.0).astype(BF16)
    lists[...] = jnp.zeros_like(lists)
    for t in range(TILES):
        inside = (local >= t * TILE) & (local < (t + 1) * TILE)
        rank = jnp.dot(before, jnp.where(inside, 1.0, 0.0).astype(BF16), preferred_element_type=F32)
        packed = jnp.where(inside & (rank.astype(jnp.int32) == slot), local * NB + number, 0)
        lists[t : t + 1, :] = jnp.sum(packed, axis=0, keepdims=True)
        lists[8 + t : 9 + t, :] = jnp.sum(jnp.where(inside, 1, 0), axis=0, keepdims=True)

    for d in (2, 6):
        pan_z[d].wait_recv()
        pan_core[d].start()
    for d in (3, 5, 4):
        pan_z[d].start()
    add_one(0)
    for d in order:
        tri_z[d].wait_recv()
        tri_core[d].start()
    add_one(1)
    left(p1)
    for d in (1, 7):
        pan_z[d].wait_recv()
        pan_core[d].start()
    add_two(0)
    add_two(1)
    left(p2)
    for d in range(8):
        tri_core[d].wait_recv()
    left([tri_z.values(), tri_core])

    @pl.when(is_root)
    def _():
        left([tri_all])

    stages = inverse_stages(tri, power, inv)
    for stage in stages[:3]:
        stage()
    last(0)
    stages[3]()
    last(1)
    left(p3)
    for d in (3, 5, 4):
        pan_z[d].wait_recv()
        pan_core[d].start()
    for stage in stages[4:]:
        stage()
    for d in range(8):
        pan_core[d].wait_recv()

    for m in range(ROWS // NB):
        w = exact(inv[...], pan[:, m * NB : (m + 1) * NB])
        if m == 0:
            w = jnp.where(is_root, -inv[...], w)
        w = jnp.transpose(w)
        hi = w.astype(BF16)
        w_hi[m * NB : (m + 1) * NB, :] = hi
        w_lo[m * NB : (m + 1) * NB, :] = (w - hi.astype(F32)).astype(BF16)

    left([pan_z.values(), pan_core])
    finish(0)
    for t in range(TILES):
        rows = pl.ds(t * TILE, TILE)
        for n, cols in enumerate((ca(0), cb(0))):
            product[rows, n * WIDE : (n + 1) * WIDE] = three_pass(w_hi[rows, :], w_lo[rows, :], top_hi[:, cols], top_lo[:, cols])
    finish(1)
    left(p4)


def exchange(pivots, matrix, panel):
    vmem = pl.BlockSpec(memory_space=pltpu.VMEM)
    hbm = pl.BlockSpec(memory_space=pltpu.HBM)
    dma = pltpu.SemaphoreType.DMA
    return pl.pallas_call(
        exchange_kernel,
        out_shape=(
            pltpu.VMEM((ROWS, COLS), F32),
            jax.ShapeDtypeStruct((16, NB), jnp.int32),
            jax.ShapeDtypeStruct((ROWS, HALF), F32),
            jax.ShapeDtypeStruct((NB, COLS), F32),
            jax.ShapeDtypeStruct((NB, COLS), BF16),
            jax.ShapeDtypeStruct((NB, COLS), BF16),
            jax.ShapeDtypeStruct((ROWS, NB), BF16),
            jax.ShapeDtypeStruct((ROWS, NB), BF16),
        ),
        in_specs=[hbm, hbm, hbm],
        out_specs=(vmem,) * 8,
        scratch_shapes=[
            pltpu.SMEM((NB,), jnp.int32),
            pltpu.VMEM((NB, WIDE), jnp.int32),
            pltpu.VMEM((NB, WIDE), jnp.int32),
            pltpu.VMEM((NB, COLS), F32),
            pltpu.VMEM((SUB, 3, 64, WIDE), F32),
            pltpu.VMEM((SUB, 3, 64, WIDE), F32),
            pltpu.VMEM((SUB, 3, 16, WIDE), F32),
            pltpu.VMEM((SUB, 3, 16, WIDE), F32),
            pltpu.VMEM((SUB, 64, WIDE), F32),
            pltpu.VMEM((SUB, 64, WIDE), F32),
            pltpu.VMEM((SUB, 64, WIDE), F32),
            pltpu.VMEM((SUB, 64, WIDE), F32),
            pltpu.VMEM((SUB, 64, WIDE), F32),
            pltpu.VMEM((SUB, 64, WIDE), F32),
            pltpu.VMEM((SUB, 4, 2, 16, WIDE), F32),
            pltpu.VMEM((SUB, 4, 2, 16, WIDE), F32),
            pltpu.VMEM((SUB, 3, 64, WIDE), F32),
            pltpu.VMEM((SUB, 3, 64, WIDE), F32),
            pltpu.VMEM((NB, ROWS), F32),
            pltpu.VMEM((NB, NB), F32),
            pltpu.VMEM((NB, NB), F32),
            pltpu.VMEM((NB, NB), F32),
            dma((3,)),
            dma((6 * SUB,)), dma((6 * SUB,)), dma((6 * SUB,)), dma((6 * SUB,)),
            dma((6 * SUB,)), dma((6 * SUB,)), dma((6 * SUB,)), dma((6 * SUB,)),
            dma((15,)), dma((1,)),
            dma((7,)), dma((7,)), dma((8,)), dma((8,)),
            dma((7,)), dma((7,)), dma((8,)), dma((8,)),
        ],
        name="exchange",
        compiler_params=pltpu.CompilerParams(
            collective_id=0, has_side_effects=True, vmem_limit_bytes=24 * 1024 * 1024
        ),
    )(*(pltpu.with_memory_space_constraint(a, pltpu.HBM) for a in (pivots, matrix, panel)))


def update_kernel(mat, lists, product, mix, th, tl, w_hi, w_lo, out_hbm, out, swaps, list_sem, out_sem):
    r = lax.axis_index("row")
    load = pltpu.make_async_copy(lists, swaps, list_sem)
    load.start()

    def store(t):
        rows = pl.ds(t * TILE, TILE)
        return pltpu.make_async_copy(out.at[rows], out_hbm.at[rows], out_sem.at[t])

    for t in range(TILES):
        rows = pl.ds(t * TILE, TILE)
        for n in range(2):
            for part in range(SUB):
                cols = pl.ds(n * HALF + part * WIDE, WIDE)
                base = mat[rows, cols]
                if t == 0:
                    base = jnp.where(r == 0, 0.0, base)
                if part == 0:
                    out[rows, cols] = base - product[rows, n * WIDE : (n + 1) * WIDE]
                else:
                    out[rows, cols] = base - three_pass(w_hi[rows, :], w_lo[rows, :], th[:, cols], tl[:, cols])
        if t == 0:
            load.wait()

        def fix(n, carry):
            entry = swaps[t, n]
            one, k = pl.ds(entry >> 8, 1), pl.ds(entry & (NB - 1), 1)
            old = jnp.where(r == 0, mat[k, :], mix[k, :])
            out[one, :] = out[one, :] + (old - mat[one, :])
            return carry

        lax.fori_loop(0, swaps[8 + t, 0], fix, 0)
        store(t).start()
    for t in range(TILES):
        store(t).wait()


def update(matrix, lists, product, mix, top_hi, top_lo, w_hi, w_lo):
    vmem = pl.BlockSpec(memory_space=pltpu.VMEM)
    anyspace = pl.BlockSpec(memory_space=pl.ANY)
    return pl.pallas_call(
        update_kernel,
        out_shape=jax.ShapeDtypeStruct((ROWS, COLS), F32),
        in_specs=[vmem, anyspace] + [vmem] * 6,
        out_specs=anyspace,
        scratch_shapes=[
            pltpu.VMEM((ROWS, COLS), F32),
            pltpu.SMEM((16, NB), jnp.int32),
            pltpu.SemaphoreType.DMA,
            pltpu.SemaphoreType.DMA((TILES,)),
        ],
        name="update",
        compiler_params=pltpu.CompilerParams(vmem_limit_bytes=24 * 1024 * 1024),
    )(matrix, lists, product, mix, top_hi, top_lo, w_hi, w_lo)


def body(matrix, lower_panel, pivots):
    return update(*exchange(pivots, matrix, lower_panel))


def solution(mesh):
    placed = (P("row", "col"), P("col", "row"), P())
    return jax.shard_map(
        body, mesh=mesh, in_specs=placed, out_specs=P("row", "col"), check_vma=False
    )
```

```python
import functools

import jax
import jax.numpy as jnp
from jax import lax
from jax.experimental import pallas as pl
from jax.experimental.pallas import tpu as pltpu
from jax.sharding import PartitionSpec as P

NB = 256
ROWS = 1536
COLS = 1024
HALF = 512
MESH = pl.DeviceIdType.MESH
F32 = jnp.float32
BF16 = jnp.bfloat16


def exact(a, b):
    return jnp.dot(a, b, preferred_element_type=F32, precision=lax.Precision.HIGHEST)


def three_pass(a_hi, a_lo, b_hi, b_lo):
    def dot(a, b):
        return jnp.dot(a, b, preferred_element_type=F32)

    return dot(a_hi, b_hi) + (dot(a_lo, b_hi) + dot(a_hi, b_lo))


def inverse_stages(tri, power, inv):
    i = lax.broadcasted_iota(jnp.int32, (NB, NB), 0)
    j = lax.broadcasted_iota(jnp.int32, (NB, NB), 1)
    eye = jnp.where(i == j, 1.0, 0.0).astype(F32)

    def begin():
        power[...] = jnp.where((j > i) & (i // 32 == j // 32), tri[...], 0.0)
        inv[...] = eye - power[...]

    def square():
        squared = exact(power[...], power[...])
        power[...] = squared
        inv[...] = exact(inv[...], eye + squared)

    def double(size):
        block = (i // (2 * size) == j // (2 * size)) & (i // size < j // size)
        inv[...] = inv[...] - exact(exact(inv[...], jnp.where(block, tri[...], 0.0)), inv[...])

    def join():
        half = NB // 2
        inv[:half, half:] = -exact(exact(inv[:half, :half], tri[:half, half:]), inv[half:, half:])

    steps = [begin, square, square, square, square]
    return steps + [functools.partial(double, size) for size in (32, 64)] + [join]


SUB = 2
TILE = 256
TILES = ROWS // TILE
WIDE = HALF // SUB


def exchange_kernel(
    piv_hbm, mat_hbm, panel_hbm, mat, lists, product, mix, top_hi, top_lo, w_hi, w_lo,
    piv, column_of, owner, sel, r1a, r1b, r2a, r2b, pa, pb, ga, gb, sa, sb, both_a, both_b, m4a, m4b, pan, tri, power, inv,
    in_sem, p1s, p1r, p2s, p2r, p3s, p3r, p4s, p4r, tbs, tbr,
    tzs, tzr, tcs, tcr, pzs, pzr, pcs, pcr,
):
    r = lax.axis_index("row")
    c = lax.axis_index("col")
    y, x = r // 4, r % 4
    z, k = c // 2, c % 2
    is_root = r == 0

    def piece(ref, zz, kk):
        return ref.at[pl.ds(pl.multiple_of((zz * 2 + kk) * 16, 16), 16)]

    my_pan = piece(pan, z, k)
    my_tri = piece(tri, z, k)
    load_pan = pltpu.make_async_copy(panel_hbm, my_pan, in_sem.at[0])
    load_piv = pltpu.make_async_copy(piv_hbm, piv, in_sem.at[1])
    load_mat = pltpu.make_async_copy(mat_hbm, mat, in_sem.at[2])
    load_pan.start()
    load_piv.start()
    load_mat.start()

    def rowdev(yy, xx):
        return (yy * 4 + xx, c)

    def coldev(zz, kk):
        return (r, zz * 2 + kk)

    barrier = pltpu.get_barrier_semaphore()
    for d in range(1, 4):
        pl.semaphore_signal(barrier, inc=1, device_id=rowdev(y, (x + d) % 4), device_id_type=MESH)
        pl.semaphore_signal(barrier, inc=1, device_id=rowdev((y + d) % 4, x), device_id_type=MESH)
    for d in range(1, 8):
        pl.semaphore_signal(barrier, inc=1, device_id=coldev((z + d) % 8, k), device_id_type=MESH)
    pl.semaphore_signal(barrier, inc=1, device_id=coldev(z, 1 - k), device_id_type=MESH)

    @pl.when((x != 0) & (y != 0))
    def _():
        pl.semaphore_signal(barrier, inc=1, device_id=(0, c), device_id_type=MESH)


    load_piv.wait()
    load_mat.wait()
    first = r * ROWS

    def pick(g, carry):
        for i in range(8):
            at = pl.ds(g * 8 + i, 1)
            pivot = piv[g * 8 + i]
            off = pivot - first
            own = (off >= 0) & (off < ROWS)
            row = mat[pl.ds(jnp.clip(off, 0, ROWS - 1), 1), :]
            sel[at, :] = jnp.where(own, row, jnp.where(is_root, mat[at, :], 0.0))
            column_of[at, :] = jnp.full((1, WIDE), pivot, jnp.int32)
        return carry

    lax.fori_loop(0, NB // 16, pick, 0)
    pl.semaphore_wait(barrier, jnp.where(is_root, 23, 14))

    def remote(src, dst, ss, rs, dev):
        return pltpu.make_async_remote_copy(
            src_ref=src, dst_ref=dst, send_sem=ss, recv_sem=rs, device_id=dev, device_id_type=MESH
        )

    def r64(i):
        return pl.ds(pl.multiple_of(i * 64, 64), 64)

    def r16(i):
        return pl.ds(pl.multiple_of(i * 16, 16), 16)

    def group(outer, inner):
        return pl.ds(pl.multiple_of(outer * 64 + inner * 16, 16), 16)

    near = (1, 3, 2)

    load_pan.wait()
    tri_all = [
        remote(my_pan.at[:, pl.ds(0, NB)], my_tri, tbs.at[d - 1], tbr.at[0], ((r + d) % 16, c)) for d in range(1, 16)
    ]

    @pl.when(is_root)
    def _():
        for cp in tri_all:
            cp.start()
        mine = pl.ds(pl.multiple_of(c * 16, 16), 16)
        tri[mine, :] = pan[mine, :NB]

    def column(ref, zs, zr, cs, cr):
        mine = piece(ref, z, k)
        along = {d: remote(mine, mine, zs.at[d - 1], zr.at[d - 1], coldev((z + d) % 8, k)) for d in range(1, 8)}
        across = []
        for d in range(8):
            got = piece(ref, (z + 8 - d) % 8, k)
            across.append(remote(got, got, cs.at[d], cr.at[d], coldev(z, 1 - k)))
        return along, across

    tri_z, tri_core = column(tri, tzs, tzr, tcs, tcr)
    pan_z, pan_core = column(pan, pzs, pzr, pcs, pcr)
    order = (1, 7, 2, 6, 3, 5, 4)
    for d, held, step in ((3, 2, 1), (5, 6, 7), (4, 2, 2)):
        got = piece(pan, (z + 8 - held) % 8, k)
        pan_z[d] = remote(got, got, pzs.at[d - 1], pzr.at[d - 1], coldev((z + step) % 8, k))
    for d in (1, 7, 2, 6):
        pan_z[d].start()
    pan_core[0].start()

    lax.fori_loop(NB // 16, NB // 8, pick, 0)
    owner[...] = ((column_of[...] >> 9) * 43691) >> 17

    def ca(s):
        return pl.ds(s * WIDE, WIDE)

    def cb(s):
        return pl.ds(HALF + s * WIDE, WIDE)

    def around(s, ss, rs, part_a, part_b, a_along_x):
        copies = []
        for d in near:
            xx, yy = (x + d) % 4, (y + d) % 4
            at, bt = s * 6 + d - 1, s * 6 + d + 2
            to_x, to_y = rowdev(y, xx), rowdev(yy, x)
            src, dst = part_a(xx if a_along_x else yy, d - 1)
            copies.append(remote(src, dst, ss.at[at], rs.at[at], to_x if a_along_x else to_y))
            src, dst = part_b(yy if a_along_x else xx, d - 1)
            copies.append(remote(src, dst, ss.at[bt], rs.at[bt], to_y if a_along_x else to_x))
        return copies

    def start(copies):
        for cp in copies:
            cp.start()

    def left(groups):
        for copies in groups:
            for cp in copies:
                cp.wait_send()

    def arrive(copies):
        for cp in copies:
            cp.wait_recv()

    p1, p2, p3, p4 = [], [], [], []
    for s in range(SUB):
        p1.append(around(
            s, p1s, p1r,
            lambda to, d: (sel.at[r64(to), ca(s)], r1a.at[s, d]),
            lambda to, d: (sel.at[r64(to), cb(s)], r1b.at[s, d]), True))
        p2.append(around(
            s, p2s, p2r,
            lambda to, d: (sa.at[s, r16(to)], r2a.at[s, d]),
            lambda to, d: (sb.at[s, r16(to)], r2b.at[s, d]), False))
        p3.append(around(
            s, p3s, p3r,
            lambda to, d: (both_a.at[s, y],) * 2,
            lambda to, d: (both_b.at[s, x],) * 2, False))
        p4.append(around(
            s, p4s, p4r,
            lambda to, d: (m4a.at[s, d], mix.at[r64(x), ca(s)]),
            lambda to, d: (m4b.at[s, d], mix.at[r64(y), cb(s)]), True))

    def total(parts, here, foreign):
        out = None
        for i, part in enumerate(parts):
            part = jnp.where(here == i, jnp.where(foreign, 0.0, part), part)
            out = part if out is None else out + part
        return out

    def one_of(parts, here):
        out = parts[3]
        for i in (2, 1, 0):
            out = jnp.where(here == i, parts[i], out)
        return out

    def add_one(s):
        arrive(p1[s])
        for cols, along, across, got, part, group_old, send, is_line in (
            (ca(s), x, y, r1a, pa, ga, sa, lambda dev: dev >> 2),
            (cb(s), y, x, r1b, pb, gb, sb, lambda dev: dev & 3),
        ):
            dev = owner[r64(along), :]
            parts = [sel[r64(along), cols], got[s, 0], got[s, 1], got[s, 2]]
            summed = total(parts, jnp.where(across == 0, along, -1), dev != 0)
            old = one_of(parts, along)
            part[s] = summed
            group_old[s] = old
            send[s] = jnp.where(is_line(dev) == 0, summed, jnp.where(across == 0, old, summed))
        start(p2[s])

    def add_two(s):
        arrive(p2[s])
        for along, across, got, part, group_old, both, is_line in (
            (x, y, r2a, pa, ga, both_a, lambda dev: dev >> 2),
            (y, x, r2b, pb, gb, both_b, lambda dev: dev & 3),
        ):
            dev = owner[group(along, across), :]
            parts = [part[s, r16(across), :], got[s, 0], got[s, 1], got[s, 2]]
            both[s, across, 0] = total(parts, jnp.where(across == 0, -1, across), is_line(dev) != 0)
            both[s, across, 1] = one_of([group_old[s, r16(across), :], parts[1], parts[2], parts[3]], across)
        start(p3[s])

    def last(s):
        arrive(p3[s])
        for cols, along, across, both, group_old, send, number in (
            (ca(s), x, y, both_a, ga, m4a, lambda to: y * 4 + to),
            (cb(s), y, x, both_b, gb, m4b, lambda to: to * 4 + x),
        ):
            dev = owner[r64(along), :]
            new = both[s, :, 0].reshape(64, WIDE)
            old = jnp.where(across == 0, group_old[s], both[s, :, 1].reshape(64, WIDE))
            for d in near:
                send[s, d - 1] = jnp.where(dev == number((along + d) % 4), old, new)
            mix[r64(along), cols] = jnp.where(dev == r, old, new)
        start(p4[s])

    def finish(s):
        arrive(p4[s])
        for cols in (ca(s), cb(s)):
            new = jnp.where(owner[...] == r, sel[:, cols], mix[:, cols])
            hi = new.astype(BF16)
            top_hi[:, cols] = hi
            top_lo[:, cols] = (new - hi.astype(F32)).astype(BF16)

    start(p1[0])
    start(p1[1])

    @pl.when(r != 0)
    def _():
        tri_all[0].wait_recv()

    for d in order:
        tri_z[d].start()
    tri_core[0].start()
    local = column_of[...] - first
    number = lax.broadcasted_iota(jnp.int32, (NB, NB), 0)
    slot = lax.broadcasted_iota(jnp.int32, (NB, NB), 1)
    before = jnp.where(number > slot, 1.0, 0.0).astype(BF16)
    lists[...] = jnp.zeros_like(lists)
    for t in range(TILES):
        inside = (local >= t * TILE) & (local < (t + 1) * TILE)
        rank = jnp.dot(before, jnp.where(inside, 1.0, 0.0).astype(BF16), preferred_element_type=F32)
        packed = jnp.where(inside & (rank.astype(jnp.int32) == slot), local * NB + number, 0)
        lists[t : t + 1, :] = jnp.sum(packed, axis=0, keepdims=True)
        lists[8 + t : 9 + t, :] = jnp.sum(jnp.where(inside, 1, 0), axis=0, keepdims=True)

    for d in (2, 6):
        pan_z[d].wait_recv()
        pan_core[d].start()
    for d in (3, 5, 4):
        pan_z[d].start()
    add_one(0)
    add_one(1)
    for d in order:
        tri_z[d].wait_recv()
        tri_core[d].start()
    left(p1)
    for d in (1, 7):
        pan_z[d].wait_recv()
        pan_core[d].start()
    add_two(0)
    add_two(1)
    left(p2)
    for d in range(8):
        tri_core[d].wait_recv()
    left([tri_z.values(), tri_core])

    @pl.when(is_root)
    def _():
        left([tri_all])

    stages = inverse_stages(tri, power, inv)
    for stage in stages[:3]:
        stage()
    last(0)
    stages[3]()
    last(1)
    left(p3)
    for d in (3, 5, 4):
        pan_z[d].wait_recv()
        pan_core[d].start()
    for stage in stages[4:]:
        stage()
    for d in range(8):
        pan_core[d].wait_recv()

    for m in range(ROWS // NB):
        w = exact(inv[...], pan[:, m * NB : (m + 1) * NB])
        if m == 0:
            w = jnp.where(is_root, -inv[...], w)
        w = jnp.transpose(w)
        hi = w.astype(BF16)
        w_hi[m * NB : (m + 1) * NB, :] = hi
        w_lo[m * NB : (m + 1) * NB, :] = (w - hi.astype(F32)).astype(BF16)

    left([pan_z.values(), pan_core])
    finish(0)
    for t in range(TILES):
        rows = pl.ds(t * TILE, TILE)
        for n, cols in enumerate((ca(0), cb(0))):
            product[rows, n * WIDE : (n + 1) * WIDE] = three_pass(w_hi[rows, :], w_lo[rows, :], top_hi[:, cols], top_lo[:, cols])
    finish(1)
    left(p4)


def exchange(pivots, matrix, panel):
    vmem = pl.BlockSpec(memory_space=pltpu.VMEM)
    hbm = pl.BlockSpec(memory_space=pltpu.HBM)
    dma = pltpu.SemaphoreType.DMA
    return pl.pallas_call(
        exchange_kernel,
        out_shape=(
            pltpu.VMEM((ROWS, COLS), F32),
            jax.ShapeDtypeStruct((16, NB), jnp.int32),
            jax.ShapeDtypeStruct((ROWS, HALF), F32),
            jax.ShapeDtypeStruct((NB, COLS), F32),
            jax.ShapeDtypeStruct((NB, COLS), BF16),
            jax.ShapeDtypeStruct((NB, COLS), BF16),
            jax.ShapeDtypeStruct((ROWS, NB), BF16),
            jax.ShapeDtypeStruct((ROWS, NB), BF16),
        ),
        in_specs=[hbm, hbm, hbm],
        out_specs=(vmem,) * 8,
        scratch_shapes=[
            pltpu.SMEM((NB,), jnp.int32),
            pltpu.VMEM((NB, WIDE), jnp.int32),
            pltpu.VMEM((NB, WIDE), jnp.int32),
            pltpu.VMEM((NB, COLS), F32),
            pltpu.VMEM((SUB, 3, 64, WIDE), F32),
            pltpu.VMEM((SUB, 3, 64, WIDE), F32),
            pltpu.VMEM((SUB, 3, 16, WIDE), F32),
            pltpu.VMEM((SUB, 3, 16, WIDE), F32),
            pltpu.VMEM((SUB, 64, WIDE), F32),
            pltpu.VMEM((SUB, 64, WIDE), F32),
            pltpu.VMEM((SUB, 64, WIDE), F32),
            pltpu.VMEM((SUB, 64, WIDE), F32),
            pltpu.VMEM((SUB, 64, WIDE), F32),
            pltpu.VMEM((SUB, 64, WIDE), F32),
            pltpu.VMEM((SUB, 4, 2, 16, WIDE), F32),
            pltpu.VMEM((SUB, 4, 2, 16, WIDE), F32),
            pltpu.VMEM((SUB, 3, 64, WIDE), F32),
            pltpu.VMEM((SUB, 3, 64, WIDE), F32),
            pltpu.VMEM((NB, ROWS), F32),
            pltpu.VMEM((NB, NB), F32),
            pltpu.VMEM((NB, NB), F32),
            pltpu.VMEM((NB, NB), F32),
            dma((3,)),
            dma((6 * SUB,)), dma((6 * SUB,)), dma((6 * SUB,)), dma((6 * SUB,)),
            dma((6 * SUB,)), dma((6 * SUB,)), dma((6 * SUB,)), dma((6 * SUB,)),
            dma((15,)), dma((1,)),
            dma((7,)), dma((7,)), dma((8,)), dma((8,)),
            dma((7,)), dma((7,)), dma((8,)), dma((8,)),
        ],
        name="exchange",
        compiler_params=pltpu.CompilerParams(
            collective_id=0, has_side_effects=True, vmem_limit_bytes=24 * 1024 * 1024
        ),
    )(*(pltpu.with_memory_space_constraint(a, pltpu.HBM) for a in (pivots, matrix, panel)))


def update_kernel(mat, lists, product, mix, th, tl, w_hi, w_lo, out_hbm, out, swaps, list_sem, out_sem):
    r = lax.axis_index("row")
    load = pltpu.make_async_copy(lists, swaps, list_sem)
    load.start()

    def store(t):
        rows = pl.ds(t * TILE, TILE)
        return pltpu.make_async_copy(out.at[rows], out_hbm.at[rows], out_sem.at[t])

    for t in range(TILES):
        rows = pl.ds(t * TILE, TILE)
        for n in range(2):
            for part in range(SUB):
                cols = pl.ds(n * HALF + part * WIDE, WIDE)
                base = mat[rows, cols]
                if t == 0:
                    base = jnp.where(r == 0, 0.0, base)
                if part == 0:
                    out[rows, cols] = base - product[rows, n * WIDE : (n + 1) * WIDE]
                else:
                    out[rows, cols] = base - three_pass(w_hi[rows, :], w_lo[rows, :], th[:, cols], tl[:, cols])
        if t == 0:
            load.wait()

        def fix(n, carry):
            entry = swaps[t, n]
            one, k = pl.ds(entry >> 8, 1), pl.ds(entry & (NB - 1), 1)
            old = jnp.where(r == 0, mat[k, :], mix[k, :])
            out[one, :] = out[one, :] + (old - mat[one, :])
            return carry

        lax.fori_loop(0, swaps[8 + t, 0], fix, 0)
        store(t).start()
    for t in range(TILES):
        store(t).wait()


def update(matrix, lists, product, mix, top_hi, top_lo, w_hi, w_lo):
    vmem = pl.BlockSpec(memory_space=pltpu.VMEM)
    anyspace = pl.BlockSpec(memory_space=pl.ANY)
    return pl.pallas_call(
        update_kernel,
        out_shape=jax.ShapeDtypeStruct((ROWS, COLS), F32),
        in_specs=[vmem, anyspace] + [vmem] * 6,
        out_specs=anyspace,
        scratch_shapes=[
            pltpu.VMEM((ROWS, COLS), F32),
            pltpu.SMEM((16, NB), jnp.int32),
            pltpu.SemaphoreType.DMA,
            pltpu.SemaphoreType.DMA((TILES,)),
        ],
        name="update",
        compiler_params=pltpu.CompilerParams(vmem_limit_bytes=24 * 1024 * 1024),
    )(matrix, lists, product, mix, top_hi, top_lo, w_hi, w_lo)


def body(matrix, lower_panel, pivots):
    return update(*exchange(pivots, matrix, lower_panel))


def solution(mesh):
    placed = (P("row", "col"), P("col", "row"), P())
    return jax.shard_map(
        body, mesh=mesh, in_specs=placed, out_specs=P("row", "col"), check_vma=False
    )
```
